32 devices in a mesh: band: 4 (over x, core), inp: 8 (over z, y).
Axes of the slice: x: 2, y: 2, z: 4, core: 2. Of those that a mesh axis runs over, the one named last changes fastest.
Arguments:
- spectra: float32 [1024, 512, 256], P('inp', 'band'), parts along dimension 1, may hold values from -6 to 6
- delays: int32 [1024], replicated, may hold values from 0 to 127
- owner_bounds: int32 [9], replicated, may hold values from 0 to 4608, as said below
Outputs:
- owned: float32 [128, 7680, 256], P('band', 'inp'), parts along dimension 0
The draws below stay inside these ranges and needn't reach their ends.
There are 4 independent parts, one for each index of `band`. The reference program is written for one: setup_inputs(seed, part) draws one part's arguments, and reference() takes and returns one part's arrays. A program takes and returns all parts, laid end to end along the dimension named above; an argument that names none is the same for every part. Nothing has to cross between parts.
Inputs may be any that keep to these rules, and one draw needn't show every extreme that they name: owner_bounds[0] = 0, owner_bounds[8] = 4608, rising; each owner_bounds[k] lies within 192 of k * 576; every owner holds at most 960 rows and some owner exactly 960.
All inputs are finite; a program needn't handle non-finite values.
Results may differ from the reference program's by a relative error of at most 0.000086.
Values sent between devices are 32-bit elements; how exact they have to be, the bound alone decides.
A program may use at most 256 MiB of HBM per device.

```python
import math
import jax
import jax.numpy as jnp
from jax import lax

SIG = 1024
CH = 128
AVG = 4
SAMP = 128
TILE = 128
BLOCK = 576
DRIFT = 192
MAXROWS = 960
N_INP = 8


def draw_owner_bounds(key, part):
    offset_key = jax.random.fold_in(key, 11)
    pick_key = jax.random.fold_in(key, 12)
    offsets = jax.random.randint(offset_key, (N_INP + 1,), -DRIFT, DRIFT + 1)
    chosen = jax.random.randint(pick_key, (), 1, N_INP - 1)
    owner_ids = jnp.arange(N_INP + 1)
    offsets = jnp.where(owner_ids == chosen, -DRIFT, offsets)
    offsets = jnp.where(owner_ids == chosen + 1, DRIFT, offsets)
    edges = (owner_ids == 0) | (owner_ids == N_INP)
    offsets = jnp.where(edges, 0, offsets)
    return (owner_ids * BLOCK + offsets).astype(jnp.int32)


def place_ends(array, stream_key, least, high):
    spot = [jax.random.randint(jax.random.fold_in(stream_key, axis), (), 0, length) for axis, length in enumerate(array.shape)]
    longest = array.shape.index(max(array.shape))
    neighbour = spot[:longest] + [(spot[longest] + 1) % array.shape[longest]] + spot[longest + 1:]
    return array.at[tuple(spot)].set(least).at[tuple(neighbour)].set(high)


def level_of(own_key, dims, split, low, high):
    level, own = 1.0, jax.random.fold_in(own_key, 6)
    for dim, shards_of in split:
        heights = jnp.exp(jax.random.uniform(jax.random.fold_in(own, dim), (shards_of,), jnp.float32, low / len(split), high / len(split)))
        level = level * jnp.repeat(heights, dims[dim] // shards_of).reshape([-1 if axis == dim else 1 for axis in range(len(dims))])
    return level


def bell_draw(stream_key, shape, deviation, limit, cuts=(), held_as=jnp.bfloat16):
    values = deviation * jax.random.normal(stream_key, shape, jnp.float32)
    if cuts:
        values = values * level_of(stream_key, shape, cuts, -0.22, 0.18)
    return jnp.clip(values, -limit, limit).astype(held_as)


def setup_inputs(seed: int = 0, part: int = 0) -> dict:
    key_list = jax.random.split(jax.random.key(seed), 4)
    own_keys = jax.random.split(jax.random.fold_in(key_list[3], part), 4)
    return {
        "spectra": bell_draw(own_keys[0], (SIG, CH, 2 * SAMP), 1.0, 6.0, ((0, 8),), jnp.float32),
        "delays": place_ends(jax.random.randint(key_list[1], (SIG,), 0, CH), jax.random.fold_in(key_list[1], 1), 0, CH - 1).astype(jnp.int32),
        "owner_bounds": draw_owner_bounds(jax.random.fold_in(key_list[3], 71), part),
    }


def cross_product(left_side, right_side):
    return lax.dot_general(left_side, right_side, (((1,), (1,)), ((), ())), precision=lax.Precision.HIGHEST, preferred_element_type=jnp.float32)


def pack_tile_rows(real_rows, imag_rows, row_tile):
    pieces = []
    for col_tile in range(row_tile + 1):
        pieces.append(jnp.concatenate([real_rows[:, col_tile * TILE:(col_tile + 1) * TILE], imag_rows[:, col_tile * TILE:(col_tile + 1) * TILE]], axis=1))
    return jnp.concatenate(pieces, axis=0)


def correct(spectra, delays, first_chan):
    inputs, local_chans, row_len = spectra.shape
    samples = row_len // 2
    channel = first_chan + jnp.arange(local_chans, dtype=jnp.int32)
    phase_steps = (delays[:, None] * channel[None, :]) % CH
    phase_angle = (phase_steps.astype(jnp.float32) * (2.0 * math.pi / CH))[:, :, None]
    cos_part = jnp.cos(phase_angle)
    sine_part = jnp.sin(phase_angle)
    real_part = spectra[:, :, :samples]
    imag_part = spectra[:, :, samples:]
    fixed_re = real_part * cos_part + imag_part * sine_part
    fixed_im = imag_part * cos_part - real_part * sine_part
    local_vis = local_chans // AVG
    direct = jnp.concatenate([fixed_re, fixed_im], axis=2).reshape(inputs, local_vis, AVG * row_len)
    swapped = jnp.concatenate([fixed_im, -fixed_re], axis=2).reshape(inputs, local_vis, AVG * row_len)
    return direct, swapped


def reference(spectra, delays, owner_bounds):
    samples = spectra.shape[2] // 2
    norm_scale = 1.0 / (AVG * samples)
    direct, swapped = correct(spectra, delays, 0)
    tile_count = SIG // TILE

    def integrate(operands):
        left_all, swap_all = operands
        square_re = cross_product(left_all, left_all) * norm_scale
        square_im = cross_product(swap_all, left_all) * norm_scale
        pieces = []
        for row_tile in range(tile_count):
            pieces.append(pack_tile_rows(square_re[row_tile * TILE:(row_tile + 1) * TILE], square_im[row_tile * TILE:(row_tile + 1) * TILE], row_tile))
        return jnp.concatenate(pieces, axis=0)

    packed = lax.map(integrate, (jnp.transpose(direct, (1, 0, 2)), jnp.transpose(swapped, (1, 0, 2))))
    counts = owner_bounds[1:] - owner_bounds[:-1]
    slot_ids = jnp.arange(MAXROWS, dtype=jnp.int32)
    is_live = slot_ids[None, :] < counts[:, None]
    row_index = jnp.where(is_live, owner_bounds[:-1, None] + slot_ids[None, :], 0).reshape(-1)
    picked = jnp.take(packed, row_index, axis=1)
    return jnp.where(is_live.reshape(-1)[None, :, None], picked, jnp.zeros_like(picked))
```

```python
import functools
import math

import jax
import jax.numpy as jnp
from jax import lax
from jax.experimental import pallas as pl
from jax.experimental.pallas import tpu as pltpu
from jax.sharding import PartitionSpec as P

CH = 128
AVG = 4
TILE = 128
GROUP = 2
MESH = pl.DeviceIdType.MESH


def correlate_kernel(
    n,
    group,
    block,
    spectra_ref,
    cos_ref,
    sin_ref,
    window_ref,
    turned,
    high,
    low,
    packed,
    x_send,
    x_recv,
    mid_send,
    low_send,
    high_send,
    mid_recv,
    low_recv,
    high_recv,
    up_send,
    down_send,
):
    me = lax.axis_index("inp")
    chunks, _, sig, cc, samples = turned.shape
    row_len = 2 * samples
    inputs = spectra_ref.shape[0]
    local_vis = packed.shape[0]
    per_chunk = local_vis // chunks
    tiles = sig // TILE
    margin = block // 3
    norm = 1.0 / (AVG * samples)

    barrier = pltpu.get_barrier_semaphore()

    def greet(d, carry):
        pl.semaphore_signal(
            barrier, inc=1, device_id={"inp": lax.rem(me + d, n)}, device_id_type=MESH
        )
        return carry

    lax.fori_loop(1, n, greet, 0)
    pl.semaphore_wait(barrier, n - 1)

    def spectra_part(chunk, half, owner, source):
        return (
            spectra_ref.at[:, owner * chunks + chunk, :, pl.ds(half * samples, samples)],
            turned.at[chunk, half, pl.ds(pl.multiple_of(source * inputs, inputs), inputs)],
        )

    def spectra_to(chunk, half, target):
        src, dst = spectra_part(chunk, half, target, me)
        return pltpu.make_async_remote_copy(
            src_ref=src,
            dst_ref=dst,
            send_sem=x_send.at[chunk, half, target],
            recv_sem=x_recv.at[chunk, half, me],
            device_id={"inp": target},
            device_id_type=MESH,
        )

    def spectra_from(chunk, half, source):
        src, dst = spectra_part(chunk, half, me, source)
        return pltpu.make_async_remote_copy(
            src_ref=src,
            dst_ref=dst,
            send_sem=x_send.at[chunk, half, source],
            recv_sem=x_recv.at[chunk, half, source],
            device_id={"inp": source},
            device_id_type=MESH,
        )

    def spectra_own(chunk, half):
        src, dst = spectra_part(chunk, half, me, me)
        return pltpu.make_async_copy(src, dst, x_recv.at[chunk, half, me])

    def start_chunk(chunk, carry):
        def start_one(d, inner):
            for half in range(2):
                spectra_to(chunk, half, lax.rem(me + d, n)).start()
            return inner

        lax.fori_loop(1, n, start_one, 0)
        for half in range(2):
            spectra_own(chunk, half).start()
        return carry

    lax.fori_loop(0, chunks, start_chunk, 0)

    pieces = (
        (margin, block, mid_send, mid_recv),
        (0, margin, low_send, low_recv),
        (margin + block, margin, high_send, high_recv),
    )

    def has_piece(index, target):
        if index == 1:
            return (target % group == 0) & (target > 0)
        if index == 2:
            return (target % group == group - 1) & (target < n - 1)
        return None

    def guarded(condition, body):
        if condition is None:
            body()
        else:
            pl.when(condition)(body)

    def remote_piece(vis, target, index):
        offset, rows, send, recv = pieces[index]
        first = target * block - margin + offset
        return pltpu.make_async_remote_copy(
            src_ref=packed.at[vis, pl.ds(pl.multiple_of(first, 8), rows)],
            dst_ref=window_ref.at[me * local_vis + vis, pl.ds(offset, rows)],
            send_sem=send.at[vis, target],
            recv_sem=recv.at[vis, me],
            device_id={"inp": target},
            device_id_type=MESH,
        )

    def arrived_piece(vis, source, index):
        offset, rows, send, recv = pieces[index]
        return pltpu.make_async_remote_copy(
            src_ref=packed.at[vis, pl.ds(0, rows)],
            dst_ref=window_ref.at[source * local_vis + vis, pl.ds(offset, rows)],
            send_sem=send.at[vis, source],
            recv_sem=recv.at[vis, source],
            device_id={"inp": lax.rem(me + 1, n)},
            device_id_type=MESH,
        )

    def own_piece(vis, index):
        offset, rows, send, recv = pieces[index]
        first = me * block - margin + offset
        return pltpu.make_async_copy(
            packed.at[vis, pl.ds(pl.multiple_of(first, 8), rows)],
            window_ref.at[me * local_vis + vis, pl.ds(offset, rows)],
            recv.at[vis, me],
        )

    def stage(vis, chunk, inner_vis):
        def stage_tile(p, carry):
            for c in range(AVG):
                first = inner_vis * AVG + c
                rows = pl.ds(pl.multiple_of(p * TILE, TILE), TILE)
                picked = pl.ds(p * TILE * cc + first, TILE, stride=cc)
                real = turned.at[chunk, 0].reshape(sig * cc, samples)[picked, :]
                imag = turned.at[chunk, 1].reshape(sig * cc, samples)[picked, :]
                cosine = cos_ref[vis, rows, c : c + 1]
                sine = sin_ref[vis, rows, c : c + 1]
                fixed_re = real * cosine + imag * sine
                fixed_im = imag * cosine - real * sine
                re_high = fixed_re.astype(jnp.bfloat16)
                im_high = fixed_im.astype(jnp.bfloat16)
                re_low = (fixed_re - re_high.astype(jnp.float32)).astype(jnp.bfloat16)
                im_low = (fixed_im - im_high.astype(jnp.float32)).astype(jnp.bfloat16)
                left = pl.ds(c * row_len, samples)
                right = pl.ds(c * row_len + samples, samples)
                for store, re_part, im_part in ((high, re_high, im_high), (low, re_low, im_low)):
                    store[p, 0:TILE, left] = re_part
                    store[p, 0:TILE, right] = im_part
                    store[p, TILE : 2 * TILE, left] = -im_part
                    store[p, TILE : 2 * TILE, right] = re_part
            return carry

        lax.fori_loop(0, tiles, stage_tile, 0)

    def multiply(vis):
        depth = AVG * row_len

        def product(a, b):
            return lax.dot_general(
                a, b, (((1,), (1,)), ((), ())), preferred_element_type=jnp.float32
            )

        def row_pair(pair, carry):
            def column(q, inner):
                both = pl.ds(2 * pair, 2)
                a_high = high[both, 0:TILE, :].reshape(2 * TILE, depth)
                a_low = low[both, 0:TILE, :].reshape(2 * TILE, depth)
                b_high = high[q]
                b_low = low[q]
                total = product(a_high, b_high)
                total += product(a_high, b_low)
                total += product(a_low, b_high)
                total *= norm
                p = 2 * pair

                @pl.when(q <= p)
                def _():
                    t = p * (p + 1) // 2 + q
                    packed[vis, pl.ds(pl.multiple_of(t * TILE, TILE), TILE), :] = total[:TILE]

                t = (p + 1) * (p + 2) // 2 + q
                packed[vis, pl.ds(pl.multiple_of(t * TILE, TILE), TILE), :] = total[TILE:]
                return inner

            lax.fori_loop(0, 2 * pair + 2, column, 0)
            return carry

        lax.fori_loop(0, tiles // 2, row_pair, 0)

    def start_rows(vis):
        def start_one(d, carry):
            target = lax.rem(me + d, n)
            for index in range(3):
                guarded(
                    has_piece(index, target),
                    lambda index=index: remote_piece(vis, target, index).start(),
                )
            return carry

        lax.fori_loop(1, n, start_one, 0)
        for index in range(3):
            guarded(has_piece(index, me), lambda index=index: own_piece(vis, index).start())

    def run_chunk(chunk, carry):
        def arrived(d, inner):
            for half in range(2):
                spectra_from(chunk, half, lax.rem(me + n - d, n)).wait_recv()
            return inner

        lax.fori_loop(1, n, arrived, 0)
        for half in range(2):
            spectra_own(chunk, half).wait()

        def run_vis(inner_vis, inner):
            vis = chunk * per_chunk + inner_vis
            stage(vis, chunk, inner_vis)
            multiply(vis)
            start_rows(vis)
            return inner

        lax.fori_loop(0, per_chunk, run_vis, 0)
        return carry

    lax.fori_loop(0, chunks, run_chunk, 0)

    def relay_up(vis, source):
        row = source * local_vis + vis
        return pltpu.make_async_remote_copy(
            src_ref=window_ref.at[row, pl.ds(block, margin)],
            dst_ref=window_ref.at[row, pl.ds(0, margin)],
            send_sem=up_send.at[vis, source],
            recv_sem=low_recv.at[vis, source],
            device_id={"inp": lax.rem(me + 1, n)},
            device_id_type=MESH,
        )

    def relay_down(vis, source):
        row = source * local_vis + vis
        return pltpu.make_async_remote_copy(
            src_ref=window_ref.at[row, pl.ds(margin, margin)],
            dst_ref=window_ref.at[row, pl.ds(margin + block, margin)],
            send_sem=down_send.at[vis, source],
            recv_sem=high_recv.at[vis, source],
            device_id={"inp": lax.rem(me + n - 1, n)},
            device_id_type=MESH,
        )

    goes_up = me % group != group - 1
    goes_down = me % group != 0

    def relay_vis(vis, carry):
        def relay_source(d, inner):
            source = lax.rem(me + n - d, n)

            @pl.when(d == 0)
            def _():
                own_piece(vis, 0).wait()

            @pl.when(d > 0)
            def _():
                arrived_piece(vis, source, 0).wait_recv()

            if group > 1:

                @pl.when(goes_up)
                def _():
                    relay_up(vis, source).start()

                @pl.when(goes_down)
                def _():
                    relay_down(vis, source).start()

            return inner

        lax.fori_loop(0, n, relay_source, 0)
        return carry

    lax.fori_loop(0, local_vis, relay_vis, 0)

    def finish_vis(vis, carry):
        def finish_one(d, inner):
            other = lax.rem(me + d, n)
            for index in range(3):
                guarded(
                    has_piece(index, other),
                    lambda index=index: remote_piece(vis, other, index).wait_send(),
                )

            @pl.when(me > 0)
            def _():
                arrived_piece(vis, other, 1).wait_recv()

            @pl.when(me < n - 1)
            def _():
                arrived_piece(vis, other, 2).wait_recv()

            return inner

        lax.fori_loop(1, n, finish_one, 0)

        @pl.when(has_piece(1, me))
        def _():
            own_piece(vis, 1).wait()

        @pl.when((me > 0) & jnp.logical_not(has_piece(1, me)))
        def _():
            arrived_piece(vis, me, 1).wait_recv()

        @pl.when(has_piece(2, me))
        def _():
            own_piece(vis, 2).wait()

        @pl.when((me < n - 1) & jnp.logical_not(has_piece(2, me)))
        def _():
            arrived_piece(vis, me, 2).wait_recv()

        if group > 1:

            def finish_relay(source, inner):
                @pl.when(goes_up)
                def _():
                    relay_up(vis, source).wait_send()

                @pl.when(goes_down)
                def _():
                    relay_down(vis, source).wait_send()

                return inner

            lax.fori_loop(0, n, finish_relay, 0)
        return carry

    lax.fori_loop(0, local_vis, finish_vis, 0)

    def finish_chunk(chunk, carry):
        def finish_spectra(d, inner):
            for half in range(2):
                spectra_to(chunk, half, lax.rem(me + d, n)).wait_send()
            return inner

        lax.fori_loop(1, n, finish_spectra, 0)
        return carry

    lax.fori_loop(0, chunks, finish_chunk, 0)


def pick_kernel(place_ref, window_ref, out_ref):
    rows = window_ref.shape[1]
    shift, count = place_ref[0], place_ref[1]
    slot = lax.broadcasted_iota(jnp.int32, window_ref.shape[1:], 0)
    back = lax.rem(rows - shift, rows)
    for b in range(window_ref.shape[0]):
        moved = pltpu.roll(window_ref[b], back, 0)
        out_ref[b] = jnp.where(slot < count, moved, 0.0)


def per_device(spectra, delays, owner_bounds):
    n = lax.axis_size("inp")
    me = lax.axis_index("inp")
    inputs, band_chans, row_len = spectra.shape
    sig = inputs * n
    local_chans = band_chans // n
    local_vis = local_chans // AVG
    all_vis = band_chans // AVG
    tiles = sig // TILE
    total_rows = tiles * (tiles + 1) // 2 * TILE
    block = total_rows // n
    margin = block // 3
    slot_rows = block + 2 * margin
    cc = min(8, local_chans)
    chunks = local_chans // cc

    channel = me * local_chans + jnp.arange(local_chans, dtype=jnp.int32)
    channel = channel.reshape(local_vis, 1, AVG)
    steps = delays[None, :, None] * channel % CH
    angle = steps.astype(jnp.float32) * (2.0 * math.pi / CH)
    cosine, sine = jnp.cos(angle), jnp.sin(angle)

    dma = lambda *shape: pltpu.SemaphoreType.DMA(shape)
    windows = pl.pallas_call(
        functools.partial(correlate_kernel, n, GROUP, block),
        out_shape=jax.ShapeDtypeStruct((all_vis, slot_rows, row_len), jnp.float32),
        in_specs=[
            pl.BlockSpec(memory_space=pl.ANY),
            pl.BlockSpec(memory_space=pltpu.VMEM),
            pl.BlockSpec(memory_space=pltpu.VMEM),
        ],
        out_specs=pl.BlockSpec(memory_space=pl.ANY),
        scratch_shapes=[
            pltpu.VMEM((chunks, 2, sig, cc, row_len // 2), jnp.float32),
            pltpu.VMEM((tiles, 2 * TILE, AVG * row_len), jnp.bfloat16),
            pltpu.VMEM((tiles, 2 * TILE, AVG * row_len), jnp.bfloat16),
            pltpu.VMEM((local_vis, total_rows, row_len), jnp.float32),
            dma(chunks, 2, n),
            dma(chunks, 2, n),
        ]
        + [dma(local_vis, n)] * 8,
        compiler_params=pltpu.CompilerParams(
            collective_id=0, has_side_effects=True, vmem_limit_bytes=60 * 1024 * 1024
        ),
    )(spectra.reshape(inputs, band_chans // cc, cc, row_len), cosine, sine)

    first = lax.dynamic_index_in_dim(owner_bounds, me, keepdims=False)
    end = lax.dynamic_index_in_dim(owner_bounds, me + 1, keepdims=False)
    place = jnp.stack([first - (me * block - margin), end - first])
    step = 2
    spec = pl.BlockSpec((step, slot_rows, row_len), lambda i, place: (i, 0, 0))
    return pl.pallas_call(
        pick_kernel,
        out_shape=jax.ShapeDtypeStruct((all_vis, slot_rows, row_len), jnp.float32),
        grid_spec=pltpu.PrefetchScalarGridSpec(
            num_scalar_prefetch=1, grid=(all_vis // step,), in_specs=[spec], out_specs=spec
        ),
        compiler_params=pltpu.CompilerParams(vmem_limit_bytes=32 * 1024 * 1024),
    )(place, windows)


def solution(mesh):
    placed = (P("inp", "band", None), P(), P())
    return jax.shard_map(
        per_device, mesh=mesh, in_specs=placed, out_specs=P("band", "inp", None), check_vma=False
    )
```

```python
import functools
import math

import jax
import jax.numpy as jnp
from jax import lax
from jax.experimental import pallas as pl
from jax.experimental.pallas import tpu as pltpu
from jax.sharding import PartitionSpec as P

CH = 128
AVG = 4
TILE = 128
MESH = pl.DeviceIdType.MESH


def correlate_kernel(
    n,
    block,
    spectra_ref,
    cos_ref,
    sin_ref,
    window_ref,
    turned,
    high,
    low,
    packed,
    x_send,
    x_recv,
    mid_send,
    low_send,
    high_send,
    mid_recv,
    low_recv,
    high_recv,
    up_send,
    down_send,
):
    me = lax.axis_index("inp")
    chunks, _, sig, cc, samples = turned.shape
    row_len = 2 * samples
    inputs = spectra_ref.shape[0]
    local_vis = packed.shape[0]
    per_chunk = local_vis // chunks
    tiles = sig // TILE
    margin = block // 3
    norm = 1.0 / (AVG * samples)

    barrier = pltpu.get_barrier_semaphore()

    def greet(d, carry):
        pl.semaphore_signal(
            barrier, inc=1, device_id={"inp": lax.rem(me + d, n)}, device_id_type=MESH
        )
        return carry

    lax.fori_loop(1, n, greet, 0)
    pl.semaphore_wait(barrier, n - 1)

    def spectra_part(chunk, half, owner, source):
        return (
            spectra_ref.at[:, owner * chunks + chunk, :, pl.ds(half * samples, samples)],
            turned.at[chunk, half, pl.ds(pl.multiple_of(source * inputs, inputs), inputs)],
        )

    def spectra_to(chunk, half, target):
        src, dst = spectra_part(chunk, half, target, me)
        return pltpu.make_async_remote_copy(
            src_ref=src,
            dst_ref=dst,
            send_sem=x_send.at[chunk, half, target],
            recv_sem=x_recv.at[chunk, half, me],
            device_id={"inp": target},
            device_id_type=MESH,
        )

    def spectra_from(chunk, half, source):
        src, dst = spectra_part(chunk, half, me, source)
        return pltpu.make_async_remote_copy(
            src_ref=src,
            dst_ref=dst,
            send_sem=x_send.at[chunk, half, source],
            recv_sem=x_recv.at[chunk, half, source],
            device_id={"inp": source},
            device_id_type=MESH,
        )

    def spectra_own(chunk, half):
        src, dst = spectra_part(chunk, half, me, me)
        return pltpu.make_async_copy(src, dst, x_recv.at[chunk, half, me])

    def start_chunk(chunk, carry):
        def start_one(d, inner):
            for half in range(2):
                spectra_to(chunk, half, lax.rem(me + 3 * d, n)).start()
            return inner

        lax.fori_loop(1, n, start_one, 0)
        for half in range(2):
            spectra_own(chunk, half).start()
        return carry

    lax.fori_loop(0, chunks, start_chunk, 0)

    pieces = (
        (margin, block, mid_send, mid_recv),
        (0, margin, low_send, low_recv),
        (margin + block, margin, high_send, high_recv),
    )

    half_axis = n // 2

    def same_half(source, target):
        return source // half_axis == target // half_axis

    def has_piece(index, source, target):
        if index == 1:
            return (target > 0) & (same_half(source, target) | (target == half_axis))
        if index == 2:
            return (target < n - 1) & (same_half(source, target) | (target == half_axis - 1))
        return None

    def guarded(condition, body):
        if condition is None:
            body()
        else:
            pl.when(condition)(body)

    def remote_piece(vis, target, index):
        offset, rows, send, recv = pieces[index]
        first = target * block - margin + offset
        return pltpu.make_async_remote_copy(
            src_ref=packed.at[vis, pl.ds(pl.multiple_of(first, 8), rows)],
            dst_ref=window_ref.at[me * local_vis + vis, pl.ds(offset, rows)],
            send_sem=send.at[vis, target],
            recv_sem=recv.at[vis, me],
            device_id={"inp": target},
            device_id_type=MESH,
        )

    def arrived_piece(vis, source, index):
        offset, rows, send, recv = pieces[index]
        return pltpu.make_async_remote_copy(
            src_ref=packed.at[vis, pl.ds(0, rows)],
            dst_ref=window_ref.at[source * local_vis + vis, pl.ds(offset, rows)],
            send_sem=send.at[vis, source],
            recv_sem=recv.at[vis, source],
            device_id={"inp": lax.rem(me + 1, n)},
            device_id_type=MESH,
        )

    def own_piece(vis, index):
        offset, rows, send, recv = pieces[index]
        first = me * block - margin + offset
        return pltpu.make_async_copy(
            packed.at[vis, pl.ds(pl.multiple_of(first, 8), rows)],
            window_ref.at[me * local_vis + vis, pl.ds(offset, rows)],
            recv.at[vis, me],
        )

    def stage(vis, chunk, inner_vis):
        def stage_tile(p, carry):
            for c in range(AVG):
                first = inner_vis * AVG + c
                rows = pl.ds(pl.multiple_of(p * TILE, TILE), TILE)
                picked = pl.ds(p * TILE * cc + first, TILE, stride=cc)
                real = turned.at[chunk, 0].reshape(sig * cc, samples)[picked, :]
                imag = turned.at[chunk, 1].reshape(sig * cc, samples)[picked, :]
                cosine = cos_ref[vis, rows, c : c + 1]
                sine = sin_ref[vis, rows, c : c + 1]
                fixed_re = real * cosine + imag * sine
                fixed_im = imag * cosine - real * sine
                re_high = fixed_re.astype(jnp.bfloat16)
                im_high = fixed_im.astype(jnp.bfloat16)
                re_low = (fixed_re - re_high.astype(jnp.float32)).astype(jnp.bfloat16)
                im_low = (fixed_im - im_high.astype(jnp.float32)).astype(jnp.bfloat16)
                left = pl.ds(c * row_len, samples)
                right = pl.ds(c * row_len + samples, samples)
                for store, re_part, im_part in ((high, re_high, im_high), (low, re_low, im_low)):
                    store[p, 0:TILE, left] = re_part
                    store[p, 0:TILE, right] = im_part
                    store[p, TILE : 2 * TILE, left] = -im_part
                    store[p, TILE : 2 * TILE, right] = re_part
            return carry

        lax.fori_loop(0, tiles, stage_tile, 0)

    def multiply(vis):
        depth = AVG * row_len

        def product(a, b):
            return lax.dot_general(
                a, b, (((1,), (1,)), ((), ())), preferred_element_type=jnp.float32
            )

        def row_pair(pair, carry):
            def column(q, inner):
                both = pl.ds(2 * pair, 2)
                a_high = high[both, 0:TILE, :].reshape(2 * TILE, depth)
                a_low = low[both, 0:TILE, :].reshape(2 * TILE, depth)
                b_high = high[q]
                b_low = low[q]
                total = product(a_high, b_high)
                total += product(a_high, b_low)
                total += product(a_low, b_high)
                total *= norm
                p = 2 * pair

                @pl.when(q <= p)
                def _():
                    t = p * (p + 1) // 2 + q
                    packed[vis, pl.ds(pl.multiple_of(t * TILE, TILE), TILE), :] = total[:TILE]

                t = (p + 1) * (p + 2) // 2 + q
                packed[vis, pl.ds(pl.multiple_of(t * TILE, TILE), TILE), :] = total[TILE:]
                return inner

            lax.fori_loop(0, 2 * pair + 2, column, 0)
            return carry

        lax.fori_loop(0, tiles // 2, row_pair, 0)

    def start_rows(vis):
        def start_one(d, carry):
            target = lax.rem(me + 3 * d, n)
            for index in range(3):
                guarded(
                    has_piece(index, me, target),
                    lambda index=index: remote_piece(vis, target, index).start(),
                )
            return carry

        lax.fori_loop(1, n, start_one, 0)
        for index in range(3):
            guarded(has_piece(index, me, me), lambda index=index: own_piece(vis, index).start())

    def relay_up(vis, source):
        row = source * local_vis + vis
        return pltpu.make_async_remote_copy(
            src_ref=window_ref.at[row, pl.ds(block, margin)],
            dst_ref=window_ref.at[row, pl.ds(0, margin)],
            send_sem=up_send.at[vis, source],
            recv_sem=low_recv.at[vis, source],
            device_id={"inp": lax.rem(me + 1, n)},
            device_id_type=MESH,
        )

    def relay_down(vis, source):
        row = source * local_vis + vis
        return pltpu.make_async_remote_copy(
            src_ref=window_ref.at[row, pl.ds(margin, margin)],
            dst_ref=window_ref.at[row, pl.ds(margin + block, margin)],
            send_sem=down_send.at[vis, source],
            recv_sem=high_recv.at[vis, source],
            device_id={"inp": lax.rem(me + n - 1, n)},
            device_id_type=MESH,
        )

    goes_up = me % half_axis != half_axis - 1
    goes_down = me % half_axis != 0

    def relay_vis(vis, carry):
        def relay_source(d, inner):
            source = lax.rem(me + (n - 3) * d, n)
            far = jnp.logical_not(same_half(source, me))

            @pl.when(far)
            def _():
                arrived_piece(vis, source, 0).wait_recv()

            @pl.when(far & goes_up)
            def _():
                relay_up(vis, source).start()

            @pl.when(far & goes_down)
            def _():
                relay_down(vis, source).start()

            return inner

        lax.fori_loop(1, n, relay_source, 0)
        return carry

    lag = max(1, local_vis - 1)

    def run_chunk(chunk, carry):
        def arrived(d, inner):
            for half in range(2):
                spectra_from(chunk, half, lax.rem(me + (n - 3) * d, n)).wait_recv()
            return inner

        lax.fori_loop(1, n, arrived, 0)
        for half in range(2):
            spectra_own(chunk, half).wait()

        def run_vis(inner_vis, inner):
            vis = chunk * per_chunk + inner_vis
            stage(vis, chunk, inner_vis)
            multiply(vis)

            @pl.when(vis >= lag)
            def _():
                relay_vis(vis - lag, 0)

            start_rows(vis)
            return inner

        lax.fori_loop(0, per_chunk, run_vis, 0)
        return carry

    lax.fori_loop(0, chunks, run_chunk, 0)

    lax.fori_loop(max(0, local_vis - lag), local_vis, relay_vis, 0)

    def finish_vis(vis, carry):
        def finish_one(d, inner):
            other = lax.rem(me + d, n)
            for index in range(3):
                guarded(
                    has_piece(index, me, other),
                    lambda index=index: remote_piece(vis, other, index).wait_send(),
                )

            @pl.when(same_half(other, me))
            def _():
                arrived_piece(vis, other, 0).wait_recv()

            @pl.when(me > 0)
            def _():
                arrived_piece(vis, other, 1).wait_recv()

            @pl.when(me < n - 1)
            def _():
                arrived_piece(vis, other, 2).wait_recv()

            return inner

        lax.fori_loop(1, n, finish_one, 0)

        for index in range(3):
            guarded(has_piece(index, me, me), lambda index=index: own_piece(vis, index).wait())

        def finish_relay(d, inner):
            source = lax.rem(me + d, n)
            far = jnp.logical_not(same_half(source, me))

            @pl.when(far & goes_up)
            def _():
                relay_up(vis, source).wait_send()

            @pl.when(far & goes_down)
            def _():
                relay_down(vis, source).wait_send()

            return inner

        lax.fori_loop(1, n, finish_relay, 0)
        return carry

    lax.fori_loop(0, local_vis, finish_vis, 0)

    def finish_chunk(chunk, carry):
        def finish_spectra(d, inner):
            for half in range(2):
                spectra_to(chunk, half, lax.rem(me + d, n)).wait_send()
            return inner

        lax.fori_loop(1, n, finish_spectra, 0)
        return carry

    lax.fori_loop(0, chunks, finish_chunk, 0)


def pick_kernel(place_ref, window_ref, out_ref):
    rows = window_ref.shape[1]
    shift, count = place_ref[0], place_ref[1]
    slot = lax.broadcasted_iota(jnp.int32, window_ref.shape[1:], 0)
    back = lax.rem(rows - shift, rows)
    for b in range(window_ref.shape[0]):
        moved = pltpu.roll(window_ref[b], back, 0)
        out_ref[b] = jnp.where(slot < count, moved, 0.0)


def per_device(spectra, delays, owner_bounds):
    n = lax.axis_size("inp")
    me = lax.axis_index("inp")
    inputs, band_chans, row_len = spectra.shape
    sig = inputs * n
    local_chans = band_chans // n
    local_vis = local_chans // AVG
    all_vis = band_chans // AVG
    tiles = sig // TILE
    total_rows = tiles * (tiles + 1) // 2 * TILE
    block = total_rows // n
    margin = block // 3
    slot_rows = block + 2 * margin
    cc = min(8, local_chans)
    chunks = local_chans // cc

    channel = me * local_chans + jnp.arange(local_chans, dtype=jnp.int32)
    steps = channel[:, None] * delays[None, :] % CH
    angle = steps.astype(jnp.float32) * (2.0 * math.pi / CH)
    tables = lax.optimization_barrier((jnp.cos(angle), jnp.sin(angle)))
    cosine, sine = (t.reshape(local_vis, AVG, sig).transpose(0, 2, 1) for t in tables)

    dma = lambda *shape: pltpu.SemaphoreType.DMA(shape)
    windows = pl.pallas_call(
        functools.partial(correlate_kernel, n, block),
        out_shape=jax.ShapeDtypeStruct((all_vis, slot_rows, row_len), jnp.float32),
        in_specs=[
            pl.BlockSpec(memory_space=pl.ANY),
            pl.BlockSpec(memory_space=pltpu.VMEM),
            pl.BlockSpec(memory_space=pltpu.VMEM),
        ],
        out_specs=pl.BlockSpec(memory_space=pl.ANY),
        scratch_shapes=[
            pltpu.VMEM((chunks, 2, sig, cc, row_len // 2), jnp.float32),
            pltpu.VMEM((tiles, 2 * TILE, AVG * row_len), jnp.bfloat16),
            pltpu.VMEM((tiles, 2 * TILE, AVG * row_len), jnp.bfloat16),
            pltpu.VMEM((local_vis, total_rows, row_len), jnp.float32),
            dma(chunks, 2, n),
            dma(chunks, 2, n),
        ]
        + [dma(local_vis, n)] * 8,
        compiler_params=pltpu.CompilerParams(
            collective_id=0, has_side_effects=True, vmem_limit_bytes=60 * 1024 * 1024
        ),
    )(spectra.reshape(inputs, band_chans // cc, cc, row_len), cosine, sine)

    first = lax.dynamic_index_in_dim(owner_bounds, me, keepdims=False)
    end = lax.dynamic_index_in_dim(owner_bounds, me + 1, keepdims=False)
    place = jnp.stack([first - (me * block - margin), end - first])
    step = 2
    spec = pl.BlockSpec((step, slot_rows, row_len), lambda i, place: (i, 0, 0))
    return pl.pallas_call(
        pick_kernel,
        out_shape=jax.ShapeDtypeStruct((all_vis, slot_rows, row_len), jnp.float32),
        grid_spec=pltpu.PrefetchScalarGridSpec(
            num_scalar_prefetch=1, grid=(all_vis // step,), in_specs=[spec], out_specs=spec
        ),
        compiler_params=pltpu.CompilerParams(vmem_limit_bytes=32 * 1024 * 1024),
    )(place, windows)


def solution(mesh):
    placed = (P("inp", "band", None), P(), P())
    return jax.shard_map(
        per_device, mesh=mesh, in_specs=placed, out_specs=P("band", "inp", None), check_vma=False
    )
```
